256 devices in a mesh: seq: 128 (over y_hi, z, x, core), ch: 2 (over y_lo).
Axes of the slice: x: 4, y: 4 (y_hi: 2, y_lo: 2; y = y_hi * 2 + y_lo), z: 8, core: 2. Of those that a mesh axis runs over, the one named last changes fastest.
Arguments:
- seq_in: bfloat16 [65536, 1536], P('seq', 'ch'), may hold values from -6 to 6
- gate_in: bfloat16 [65536, 1536], P('seq', 'ch'), may hold values from -6 to 6
- first_blocks: bfloat16 [128, 512, 512], P('seq'), may hold values from -0.25 to 0.25
- second_blocks: bfloat16 [512, 128, 128], P('seq'), may hold values from -0.5 to 0.5
- out_weight: bfloat16 [1536, 1536], P(None, 'ch'), may hold values from -0.15625 to 0.15625
- cotangent: bfloat16 [65536, 1536], P('seq', 'ch'), may hold values from -6 to 6
Outputs:
- result: bfloat16 [65536, 1536], P('seq', 'ch')
- grad_in: bfloat16 [65536, 1536], P('seq', 'ch')
The draws below stay inside these ranges and needn't reach their ends.
All inputs are finite; a program needn't handle non-finite values.
Results may differ from the reference program's by a relative error of at most 0.018.
Values may be sent and summed in bfloat16 or wider, within the bound.
A program may use at most 64 MiB of HBM per device.

```python
import jax
import jax.numpy as jnp

D = 1536
BLOCK = 512
NCHUNK = 128
LENGTH = 65536


def block_levels(own_key, extent, pieces, smallest, top_value):
    gain, own = 1.0, jax.random.fold_in(own_key, 6)
    for axis_at, blocks in pieces:
        draws = jnp.exp(jax.random.uniform(jax.random.fold_in(own, axis_at), (blocks,), jnp.float32, smallest / len(pieces), top_value / len(pieces)))
        gain = gain * jnp.repeat(draws, extent[axis_at] // blocks).reshape([-1 if axis == axis_at else 1 for axis in range(len(extent))])
    return gain


def scatter_about(key, dims, spread, limit, split=(), held_as=jnp.bfloat16):
    entries = jax.random.normal(key, dims, jnp.float32) * spread
    if len(split) > 0:
        entries = block_levels(key, dims, split, -0.22, 0.18) * entries
    return jnp.clip(entries, min=-limit, max=limit).astype(held_as)


def setup_inputs(seed: int = 0) -> dict:
    key_of = jax.random.split(jax.random.key(seed), 7)
    seq_in = scatter_about(key_of[0], (LENGTH, D), 1.0, 6.0, ((0, 128), (1, 2)))
    gate_in = scatter_about(key_of[1], (LENGTH, D), 1.5, 6.0, ((0, 128), (1, 2)))
    first_blocks = scatter_about(key_of[2], (NCHUNK, BLOCK, BLOCK), BLOCK ** -0.5, 0.25, ((0, 128),))
    second_blocks = scatter_about(key_of[3], (BLOCK, NCHUNK, NCHUNK), NCHUNK ** -0.5, 0.5, ((0, 128),))
    out_weight = scatter_about(key_of[4], (D, D), D ** -0.5, 0.15625, ((1, 2),))
    cotangent = scatter_about(key_of[5], (LENGTH, D), 1.0, 6.0, ((0, 128), (1, 2)))
    return {"seq_in": seq_in, "gate_in": gate_in, "first_blocks": first_blocks, "second_blocks": second_blocks, "out_weight": out_weight, "cotangent": cotangent}


def reference(seq_in, gate_in, first_blocks, second_blocks, out_weight, cotangent):
    blocks_one = first_blocks.astype(jnp.float32)
    blocks_two = second_blocks.astype(jnp.float32)
    inputs = seq_in.reshape(NCHUNK, BLOCK, D).astype(jnp.float32)
    first = jnp.einsum('cij,cjd->cid', blocks_one, inputs).astype(jnp.bfloat16)
    mixed = jnp.einsum('icj,jid->cid', blocks_two, first.astype(jnp.float32)).astype(jnp.bfloat16)
    gate = jax.nn.silu(gate_in.reshape(NCHUNK, BLOCK, D).astype(jnp.float32))
    gated = (mixed.astype(jnp.float32) * gate).astype(jnp.bfloat16)
    result = jnp.dot(gated.reshape(LENGTH, D), out_weight, preferred_element_type=jnp.float32).astype(jnp.bfloat16)
    grad_gated = jnp.dot(cotangent, out_weight.T, preferred_element_type=jnp.float32).astype(jnp.bfloat16)
    grad_mixed = (grad_gated.reshape(NCHUNK, BLOCK, D).astype(jnp.float32) * gate).astype(jnp.bfloat16)
    grad_first = jnp.einsum('icj,cid->jid', blocks_two, grad_mixed.astype(jnp.float32)).astype(jnp.bfloat16)
    grad_in = jnp.einsum('cij,cid->cjd', blocks_one, grad_first.astype(jnp.float32)).astype(jnp.bfloat16)
    return result, grad_in.reshape(LENGTH, D)
```

```python
import jax
import jax.numpy as jnp
from jax import lax
from jax.experimental import pallas as pl
from jax.experimental.pallas import tpu as pltpu
from jax.sharding import PartitionSpec as P

MESH = pl.DeviceIdType.MESH
SEQ = 128
CHIPS = SEQ // 2
ROWS = 8
BLOCK = 512
WIDTH = 768
HALF = WIDTH // 2
COLS = HALF // 128
F32 = jnp.float32
BF16 = jnp.bfloat16


def dot(a, b, ca=1, cb=0):
    return lax.dot_general(a, b, (((ca,), (cb,)), ((), ())), preferred_element_type=F32)


def kernel(
    seq_hbm, gate_hbm, first_hbm, second_hbm, weight_hbm, cot_hbm,
    result_ref, grad_ref,
    seq, gate_in, blocks, second, weight, cot,
    gate, own_part, part_send, part_recv,
    a_send, a_recv, m_send, a_ret,
    b_send, b_recv, g_send, b_ret,
    wide, wide_out, gated, gated_other, total,
    load_sem, second_sem, part_sem, gated_sem, send_sem, recv_sem, a_ret_sem, b_ret_sem,
):
    me = lax.axis_index("seq")
    ch = lax.axis_index("ch")
    chip, core = me // 2, lax.rem(me, 2)
    partner = me + 1 - 2 * core
    across = {"ch": 1 - ch}
    hub = core * CHIPS + chip

    loads = [
        pltpu.make_async_copy(src, dst, load_sem.at[k])
        for k, (src, dst) in enumerate(
            [
                (first_hbm, blocks),
                (seq_hbm, seq),
                (cot_hbm, cot),
                (weight_hbm, weight),
                (gate_hbm, gate_in),
                (second_hbm, second.at[pl.ds(core * 4, 4)]),
            ]
        )
    ]
    for load in loads:
        load.start()

    barrier = pltpu.get_barrier_semaphore()

    @pl.loop(1, SEQ)
    def _(s):
        pl.semaphore_signal(
            barrier, inc=1, device_id={"seq": lax.rem(me + s, SEQ)}, device_id_type=MESH
        )

    pl.semaphore_signal(barrier, inc=1, device_id=across, device_id_type=MESH)

    def columns(j):
        return pl.ds(j * HALF, HALF)

    def slots(j):
        return pl.ds(j * CHIPS, CHIPS)

    loads[0].wait()
    loads[1].wait()
    for j in range(2):
        part = dot(blocks[0], seq[:, columns(j)])
        a_send[slots(j)] = part.reshape(CHIPS, ROWS, HALF).astype(BF16)
    loads[2].wait()
    loads[3].wait()
    for j in range(2):
        rows = weight[pl.ds(pl.multiple_of((1 - ch) * WIDTH + j * HALF, HALF), HALF), :]
        part_send[j] = dot(cot[...], rows, 1, 1).astype(BF16)
    loads[5].wait()

    pl.semaphore_wait(barrier, SEQ)

    def across_copy(src, dst, sems, j):
        return pltpu.make_async_remote_copy(
            src, dst, sems.at[j], sems.at[2 + j], device_id=across, device_id_type=MESH
        )

    def to_peer(src, dst, send, recv, peer):
        return pltpu.make_async_remote_copy(
            src, dst, send, recv, device_id={"seq": peer}, device_id_type=MESH
        )

    def spread(send, recv, k, j):
        @pl.loop(1, CHIPS)
        def _(s):
            t = lax.rem(chip + s, CHIPS)
            to_peer(
                send.at[j * CHIPS + t], recv.at[me], send_sem.at[k], recv_sem.at[k], 2 * t + j
            ).start()

    def spread_near(send, recv, k):
        to_peer(
            send.at[(1 - core) * CHIPS + chip], recv.at[me], send_sem.at[k], recv_sem.at[k], partner
        ).start()
        pltpu.make_async_copy(send.at[hub], recv.at[me], recv_sem.at[k]).start()

    def give_back(send, recv, k, sems):
        @pl.loop(1, SEQ)
        def _(s):
            peer = lax.rem(me + s, SEQ)
            to_peer(send.at[peer], recv.at[hub], send_sem.at[k], sems.at[core], peer).start()

        pltpu.make_async_copy(send.at[me], recv.at[hub], sems.at[core]).start()

    def wait_all(ref, sem):
        pltpu.make_async_copy(ref, ref, sem).wait()

    def mix(recv, send, back):
        for k in range(COLS):
            lanes = pl.ds(k * 128, 128)
            wide[k] = recv[:, :, lanes].astype(F32).reshape(SEQ * ROWS, 128)
        for i in range(ROWS):
            at = pl.ds(i, SEQ, stride=ROWS)
            rows = [wide[k, at, :].astype(BF16) for k in range(COLS)]
            part = dot(second[i], jnp.concatenate(rows, axis=1), 0 if back else 1, 0)
            for k in range(COLS):
                wide_out[k, at, :] = part[:, k * 128 : (k + 1) * 128]
        for k in range(COLS):
            lanes = pl.ds(k * 128, 128)
            send[:, :, lanes] = wide_out[k].reshape(SEQ, ROWS, 128).astype(BF16)

    share = to_peer(
        second.at[pl.ds(core * 4, 4)],
        second.at[pl.ds(core * 4, 4)],
        second_sem.at[0],
        second_sem.at[1],
        partner,
    )
    share.start()
    parts = [across_copy(part_send.at[j], part_recv.at[j], part_sem, j) for j in range(2)]
    for copy in parts:
        copy.start()
    spread(a_send, a_recv, 0, 0)
    spread(a_send, a_recv, 0, 1)
    spread_near(a_send, a_recv, 0)

    loads[4].wait()
    for j in range(2):
        value = gate_in[:, columns(j)].astype(F32)
        gate[:, columns(j)] = value / (1.0 + jnp.exp(-value))
        rows = weight[pl.ds(pl.multiple_of(ch * WIDTH + j * HALF, HALF), HALF), :]
        own_part[:, columns(j)] = dot(cot[...], rows, 1, 1)

    for j in range(2):
        parts[j].wait_recv()
        grad_gated = (own_part[:, columns(j)] + part_recv[j].astype(F32)).astype(BF16)
        grad_mixed = grad_gated.astype(F32) * gate[:, columns(j)]
        b_send[slots(j)] = grad_mixed.reshape(CHIPS, ROWS, HALF).astype(BF16)
        spread(b_send, b_recv, 1, j)
    spread_near(b_send, b_recv, 1)

    share.wait_recv()
    wait_all(a_recv, recv_sem.at[0])
    mix(a_recv, m_send, False)
    give_back(m_send, a_ret, 2, a_ret_sem)

    wait_all(b_recv, recv_sem.at[1])
    mix(b_recv, g_send, True)
    give_back(g_send, b_ret, 3, b_ret_sem)

    gates = [across_copy(gated.at[j], gated_other.at[j], gated_sem, j) for j in range(2)]
    for j in range(2):
        wait_all(a_ret.at[slots(j)], a_ret_sem.at[j])
        mixed = a_ret[slots(j)].astype(F32).reshape(BLOCK, HALF)
        gated[j] = (mixed * gate[:, columns(j)]).astype(BF16)
        gates[j].start()
    for j in range(2):
        rows = weight[pl.ds(pl.multiple_of(ch * WIDTH + j * HALF, HALF), HALF), :]
        if j == 0:
            total[...] = dot(gated[j], rows)
        else:
            total[...] += dot(gated[j], rows)

    for j in range(2):
        wait_all(b_ret.at[slots(j)], b_ret_sem.at[j])
        grad_first = b_ret[slots(j)].astype(F32).reshape(BLOCK, HALF).astype(BF16)
        grad_ref[:, columns(j)] = dot(blocks[0], grad_first, 0, 0).astype(BF16)

    for j in range(2):
        gates[j].wait_recv()
        rows = weight[pl.ds(pl.multiple_of((1 - ch) * WIDTH + j * HALF, HALF), HALF), :]
        if j == 0:
            total[...] += dot(gated_other[j], rows)
        else:
            result_ref[...] = (total[...] + dot(gated_other[j], rows)).astype(BF16)

    for j in range(2):
        parts[j].wait_send()
        gates[j].wait_send()
    share.wait_send()
    for k, ref in enumerate((a_send, b_send, m_send, g_send)):
        sent = ref.at[pl.ds(0, SEQ - 1)]
        wait_all(sent, send_sem.at[k])


def body(seq_in, gate_in, first_blocks, second_blocks, out_weight, cotangent):
    whole = pltpu.VMEM((BLOCK, WIDTH), BF16)
    whole_f32 = pltpu.VMEM((BLOCK, WIDTH), F32)
    halves = pltpu.VMEM((2, BLOCK, HALF), BF16)
    messages = pltpu.VMEM((SEQ, ROWS, HALF), BF16)
    wide = pltpu.VMEM((COLS, SEQ * ROWS, 128), F32)
    dma = pltpu.SemaphoreType.DMA
    out = jax.ShapeDtypeStruct((BLOCK, WIDTH), BF16)
    return pl.pallas_call(
        kernel,
        out_shape=(out, out),
        in_specs=[pl.BlockSpec(memory_space=pl.ANY)] * 6,
        out_specs=(pl.BlockSpec(memory_space=pltpu.VMEM),) * 2,
        scratch_shapes=[
            whole,
            whole,
            pltpu.VMEM((1, BLOCK, BLOCK), BF16),
            pltpu.VMEM((ROWS, SEQ, SEQ), BF16),
            pltpu.VMEM((2 * WIDTH, WIDTH), BF16),
            whole,
            whole_f32,
            whole_f32,
            halves,
            halves,
        ]
        + [messages] * 8
        + [wide, wide, halves, halves, whole_f32]
        + [dma((6,)), dma((2,)), dma((4,)), dma((4,)), dma((4,)), dma((2,)), dma((2,)), dma((2,))],
        compiler_params=pltpu.CompilerParams(
            collective_id=0, has_side_effects=True, vmem_limit_bytes=62 * 2**20
        ),
        cost_estimate=pl.CostEstimate(
            flops=3_500_000_000, bytes_accessed=7_000_000, transcendentals=400_000
        ),
        name="monarch",
    )(seq_in, gate_in, first_blocks, second_blocks, out_weight, cotangent)


def solution(mesh):
    return jax.shard_map(
        body,
        mesh=mesh,
        in_specs=(
            P("seq", "ch"),
            P("seq", "ch"),
            P("seq", None, None),
            P("seq", None, None),
            P(None, "ch"),
            P("seq", "ch"),
        ),
        out_specs=(P("seq", "ch"), P("seq", "ch")),
        check_vma=False,
    )
```

```python
import jax
import jax.numpy as jnp
from jax import lax
from jax.experimental import pallas as pl
from jax.experimental.pallas import tpu as pltpu
from jax.sharding import PartitionSpec as P

MESH = pl.DeviceIdType.MESH
SEQ = 128
CHIPS = SEQ // 2
ROWS = 8
BLOCK = 512
WIDTH = 768
HALF = WIDTH // 2
COLS = HALF // 128
F32 = jnp.float32
BF16 = jnp.bfloat16


def dot(a, b, ca=1, cb=0):
    return lax.dot_general(a, b, (((ca,), (cb,)), ((), ())), preferred_element_type=F32)


def kernel(
    seq_hbm, gate_hbm, first_hbm, second_hbm, weight_hbm, cot_hbm,
    result_ref, grad_ref,
    seq, gate_in, blocks, second, weight, cot,
    gate, own_part, part_send, part_recv,
    a_send, a_recv, m_send, a_ret,
    b_send, b_recv, g_send, b_ret,
    wide, wide_out, gated, gated_other, total,
    load_sem, second_sem, part_sem, gated_sem, send_sem, recv_sem, a_ret_sem, b_ret_sem,
):
    me = lax.axis_index("seq")
    ch = lax.axis_index("ch")
    chip, core = me // 2, lax.rem(me, 2)
    partner = me + 1 - 2 * core
    across = {"ch": 1 - ch}
    hub = core * CHIPS + chip

    loads = [
        pltpu.make_async_copy(src, dst, load_sem.at[k])
        for k, (src, dst) in enumerate(
            [
                (first_hbm, blocks),
                (seq_hbm, seq),
                (cot_hbm, cot),
                (weight_hbm, weight),
                (gate_hbm, gate_in),
                (second_hbm, second.at[pl.ds(core * 4, 4)]),
            ]
        )
    ]
    for load in loads:
        load.start()

    barrier = pltpu.get_barrier_semaphore()

    @pl.loop(1, SEQ)
    def _(s):
        pl.semaphore_signal(
            barrier, inc=1, device_id={"seq": lax.rem(me + s, SEQ)}, device_id_type=MESH
        )

    pl.semaphore_signal(barrier, inc=1, device_id=across, device_id_type=MESH)

    def columns(j):
        return pl.ds(j * HALF, HALF)

    def slots(j):
        return pl.ds(j * CHIPS, CHIPS)

    loads[0].wait()
    loads[1].wait()
    for j in range(2):
        part = dot(blocks[0], seq[:, columns(j)])
        a_send[slots(j)] = part.reshape(CHIPS, ROWS, HALF).astype(BF16)
    loads[2].wait()
    loads[3].wait()
    for j in range(2):
        rows = weight[pl.ds(pl.multiple_of((1 - ch) * WIDTH + j * HALF, HALF), HALF), :]
        part_send[j] = dot(cot[...], rows, 1, 1).astype(BF16)
    loads[5].wait()

    pl.semaphore_wait(barrier, SEQ)

    def across_copy(src, dst, sems, j):
        return pltpu.make_async_remote_copy(
            src, dst, sems.at[j], sems.at[2 + j], device_id=across, device_id_type=MESH
        )

    def to_peer(src, dst, send, recv, peer):
        return pltpu.make_async_remote_copy(
            src, dst, send, recv, device_id={"seq": peer}, device_id_type=MESH
        )

    def spread(send, recv, k, j):
        @pl.loop(1, CHIPS)
        def _(s):
            t = lax.rem(chip + s, CHIPS)
            to_peer(
                send.at[j * CHIPS + t], recv.at[me], send_sem.at[k], recv_sem.at[k], 2 * t + j
            ).start()

    def spread_near(send, recv, k):
        to_peer(
            send.at[(1 - core) * CHIPS + chip], recv.at[me], send_sem.at[k], recv_sem.at[k], partner
        ).start()
        pltpu.make_async_copy(send.at[hub], recv.at[me], recv_sem.at[k]).start()

    def give_back(send, recv, k, sems):
        @pl.loop(1, SEQ)
        def _(s):
            peer = lax.rem(me + s, SEQ)
            to_peer(send.at[peer], recv.at[hub], send_sem.at[k], sems.at[core], peer).start()

        pltpu.make_async_copy(send.at[me], recv.at[hub], sems.at[core]).start()

    def wait_all(ref, sem):
        pltpu.make_async_copy(ref, ref, sem).wait()

    def mix(recv, send, back):
        for k in range(COLS):
            lanes = pl.ds(k * 128, 128)
            wide[k] = recv[:, :, lanes].astype(F32).reshape(SEQ * ROWS, 128)
        for i in range(ROWS):
            at = pl.ds(i, SEQ, stride=ROWS)
            rows = [wide[k, at, :].astype(BF16) for k in range(COLS)]
            part = dot(second[i], jnp.concatenate(rows, axis=1), 0 if back else 1, 0)
            for k in range(COLS):
                wide_out[k, at, :] = part[:, k * 128 : (k + 1) * 128]
        for k in range(COLS):
            lanes = pl.ds(k * 128, 128)
            send[:, :, lanes] = wide_out[k].reshape(SEQ, ROWS, 128).astype(BF16)

    share = to_peer(
        second.at[pl.ds(core * 4, 4)],
        second.at[pl.ds(core * 4, 4)],
        second_sem.at[0],
        second_sem.at[1],
        partner,
    )
    share.start()
    parts = [across_copy(part_send.at[j], part_recv.at[j], part_sem, j) for j in range(2)]
    parts[0].start()
    spread(a_send, a_recv, 0, 0)
    spread(a_send, a_recv, 0, 1)
    spread_near(a_send, a_recv, 0)

    loads[4].wait()
    for j in range(2):
        value = gate_in[:, columns(j)].astype(F32)
        gate[:, columns(j)] = value / (1.0 + jnp.exp(-value))
        rows = weight[pl.ds(pl.multiple_of(ch * WIDTH + j * HALF, HALF), HALF), :]
        own_part[:, columns(j)] = dot(cot[...], rows, 1, 1)

    def send_grad(j):
        parts[j].wait_recv()
        if j == 0:
            parts[1].start()
        grad_gated = (own_part[:, columns(j)] + part_recv[j].astype(F32)).astype(BF16)
        grad_mixed = grad_gated.astype(F32) * gate[:, columns(j)]
        b_send[slots(j)] = grad_mixed.reshape(CHIPS, ROWS, HALF).astype(BF16)
        spread(b_send, b_recv, 1, j)

    send_grad(0)
    share.wait_recv()
    wait_all(a_recv, recv_sem.at[0])
    mix(a_recv, m_send, False)
    give_back(m_send, a_ret, 2, a_ret_sem)
    send_grad(1)
    spread_near(b_send, b_recv, 1)

    wait_all(b_recv, recv_sem.at[1])
    mix(b_recv, g_send, True)
    give_back(g_send, b_ret, 3, b_ret_sem)

    gates = [across_copy(gated.at[j], gated_other.at[j], gated_sem, j) for j in range(2)]
    for j in range(2):
        wait_all(a_ret.at[slots(j)], a_ret_sem.at[j])
        mixed = a_ret[slots(j)].astype(F32).reshape(BLOCK, HALF)
        gated[j] = (mixed * gate[:, columns(j)]).astype(BF16)
        gates[j].start()
    for j in range(2):
        rows = weight[pl.ds(pl.multiple_of(ch * WIDTH + j * HALF, HALF), HALF), :]
        if j == 0:
            total[...] = dot(gated[j], rows)
        else:
            total[...] += dot(gated[j], rows)

    for j in range(2):
        wait_all(b_ret.at[slots(j)], b_ret_sem.at[j])
        grad_first = b_ret[slots(j)].astype(F32).reshape(BLOCK, HALF).astype(BF16)
        grad_ref[:, columns(j)] = dot(blocks[0], grad_first, 0, 0).astype(BF16)

    for j in range(2):
        gates[j].wait_recv()
        rows = weight[pl.ds(pl.multiple_of((1 - ch) * WIDTH + j * HALF, HALF), HALF), :]
        if j == 0:
            total[...] += dot(gated_other[j], rows)
        else:
            result_ref[...] = (total[...] + dot(gated_other[j], rows)).astype(BF16)

    for j in range(2):
        parts[j].wait_send()
        gates[j].wait_send()
    share.wait_send()
    for k, ref in enumerate((a_send, b_send, m_send, g_send)):
        sent = ref.at[pl.ds(0, SEQ - 1)]
        wait_all(sent, send_sem.at[k])


def body(seq_in, gate_in, first_blocks, second_blocks, out_weight, cotangent):
    whole = pltpu.VMEM((BLOCK, WIDTH), BF16)
    whole_f32 = pltpu.VMEM((BLOCK, WIDTH), F32)
    halves = pltpu.VMEM((2, BLOCK, HALF), BF16)
    messages = pltpu.VMEM((SEQ, ROWS, HALF), BF16)
    wide = pltpu.VMEM((COLS, SEQ * ROWS, 128), F32)
    dma = pltpu.SemaphoreType.DMA
    out = pltpu.VMEM((BLOCK, WIDTH), BF16)
    return pl.pallas_call(
        kernel,
        out_shape=(out, out),
        in_specs=[pl.BlockSpec(memory_space=pl.ANY)] * 6,
        out_specs=(pl.BlockSpec(memory_space=pltpu.VMEM),) * 2,
        scratch_shapes=[
            whole,
            whole,
            pltpu.VMEM((1, BLOCK, BLOCK), BF16),
            pltpu.VMEM((ROWS, SEQ, SEQ), BF16),
            pltpu.VMEM((2 * WIDTH, WIDTH), BF16),
            whole,
            whole_f32,
            whole_f32,
            halves,
            halves,
        ]
        + [messages] * 8
        + [wide, wide, halves, halves, whole_f32]
        + [dma((6,)), dma((2,)), dma((4,)), dma((4,)), dma((4,)), dma((2,)), dma((2,)), dma((2,))],
        compiler_params=pltpu.CompilerParams(
            collective_id=0, has_side_effects=True, vmem_limit_bytes=60 * 2**20
        ),
        cost_estimate=pl.CostEstimate(
            flops=3_500_000_000, bytes_accessed=7_000_000, transcendentals=400_000
        ),
        name="monarch",
    )(seq_in, gate_in, first_blocks, second_blocks, out_weight, cotangent)


def solution(mesh):
    return jax.shard_map(
        body,
        mesh=mesh,
        in_specs=(
            P("seq", "ch"),
            P("seq", "ch"),
            P("seq", None, None),
            P("seq", None, None),
            P(None, "ch"),
            P("seq", "ch"),
        ),
        out_specs=(P("seq", "ch"), P("seq", "ch")),
        check_vma=False,
    )
```

```python
import jax
import jax.numpy as jnp
from jax import lax
from jax.experimental import pallas as pl
from jax.experimental.pallas import tpu as pltpu
from jax.sharding import PartitionSpec as P

MESH = pl.DeviceIdType.MESH
SEQ = 128
CHIPS = SEQ // 2
ROWS = 8
BLOCK = 512
WIDTH = 768
HALF = WIDTH // 2
COLS = HALF // 128
F32 = jnp.float32
BF16 = jnp.bfloat16


def dot(a, b, ca=1, cb=0):
    return lax.dot_general(a, b, (((ca,), (cb,)), ((), ())), preferred_element_type=F32)


def kernel(
    seq_hbm, gate_hbm, first_hbm, second_hbm, weight_hbm, cot_hbm,
    result_ref, grad_ref,
    seq, gate_in, blocks, second, weight, cot,
    gate, own_part, part_send, part_recv,
    a_send, a_recv, m_send, a_ret,
    b_send, b_recv, g_send, b_ret,
    wide, wide_out, gated, gated_other, total, blocks_t,
    load_sem, second_sem, part_sem, gated_sem, send_sem, recv_sem, a_ret_sem, b_ret_sem,
):
    me = lax.axis_index("seq")
    ch = lax.axis_index("ch")
    chip, core = me // 2, lax.rem(me, 2)
    partner = me + 1 - 2 * core
    across = {"ch": 1 - ch}
    hub = core * CHIPS + chip

    loads = [
        pltpu.make_async_copy(src, dst, load_sem.at[k])
        for k, (src, dst) in enumerate(
            [
                (first_hbm, blocks),
                (seq_hbm, seq),
                (cot_hbm, cot),
                (weight_hbm, weight),
                (gate_hbm, gate_in),
                (second_hbm, second.at[pl.ds(core * 4, 4)]),
            ]
        )
    ]
    for load in loads:
        load.start()

    barrier = pltpu.get_barrier_semaphore()

    @pl.loop(1, SEQ)
    def _(s):
        pl.semaphore_signal(
            barrier, inc=1, device_id={"seq": lax.rem(me + s, SEQ)}, device_id_type=MESH
        )

    pl.semaphore_signal(barrier, inc=1, device_id=across, device_id_type=MESH)

    def columns(j):
        return pl.ds(j * HALF, HALF)

    def slots(j):
        return pl.ds(j * CHIPS, CHIPS)

    loads[0].wait()
    loads[1].wait()
    for j in range(2):
        part = dot(blocks[0], seq[:, columns(j)])
        a_send[slots(j)] = part.reshape(CHIPS, ROWS, HALF).astype(BF16)
    loads[2].wait()
    loads[3].wait()
    for j in range(2):
        rows = weight[pl.ds(pl.multiple_of((1 - ch) * WIDTH + j * HALF, HALF), HALF), :]
        part_send[j] = dot(cot[...], rows, 1, 1).astype(BF16)
    loads[5].wait()

    pl.semaphore_wait(barrier, SEQ)

    def across_copy(src, dst, sems, j):
        return pltpu.make_async_remote_copy(
            src, dst, sems.at[j], sems.at[2 + j], device_id=across, device_id_type=MESH
        )

    def to_peer(src, dst, send, recv, peer):
        return pltpu.make_async_remote_copy(
            src, dst, send, recv, device_id={"seq": peer}, device_id_type=MESH
        )

    def spread(send, recv, k, j):
        @pl.loop(1, CHIPS, unroll=7)
        def _(s):
            t = lax.rem(chip + s, CHIPS)
            to_peer(
                send.at[j * CHIPS + t], recv.at[me], send_sem.at[k], recv_sem.at[k], 2 * t + j
            ).start()

        slot = j * CHIPS + chip

        @pl.when(core == j)
        def _():
            pltpu.make_async_copy(send.at[slot], recv.at[me], recv_sem.at[k]).start()

        @pl.when(core != j)
        def _():
            to_peer(send.at[slot], recv.at[me], send_sem.at[k], recv_sem.at[k], partner).start()

    def give_back(send, recv, k, sems):
        @pl.loop(1, CHIPS, unroll=7)
        def _(s):
            t = lax.rem(chip + s, CHIPS)
            for j in range(2):
                peer = 2 * t + j
                to_peer(send.at[peer], recv.at[hub], send_sem.at[k], sems.at[core], peer).start()

        to_peer(send.at[partner], recv.at[hub], send_sem.at[k], sems.at[core], partner).start()

        pltpu.make_async_copy(send.at[me], recv.at[hub], sems.at[core]).start()

    def wait_all(ref, sem):
        pltpu.make_async_copy(ref, ref, sem).wait()

    def mix(recv, send, back):
        for k in range(COLS):
            lanes = pl.ds(k * 128, 128)
            wide[k] = recv[:, :, lanes].astype(F32).reshape(SEQ * ROWS, 128)
        for i in range(ROWS):
            at = pl.ds(i, SEQ, stride=ROWS)
            rows = [wide[k, at, :].astype(BF16) for k in range(COLS)]
            part = dot(second[i], jnp.concatenate(rows, axis=1), 0 if back else 1, 0)
            for k in range(COLS):
                wide_out[k, at, :] = part[:, k * 128 : (k + 1) * 128]
        for k in range(COLS):
            lanes = pl.ds(k * 128, 128)
            send[:, :, lanes] = wide_out[k].reshape(SEQ, ROWS, 128).astype(BF16)

    share = to_peer(
        second.at[pl.ds(core * 4, 4)],
        second.at[pl.ds(core * 4, 4)],
        second_sem.at[0],
        second_sem.at[1],
        partner,
    )
    share.start()
    parts = [across_copy(part_send.at[j], part_recv.at[j], part_sem, j) for j in range(2)]
    parts[0].start()
    spread(a_send, a_recv, 0, 0)
    spread(a_send, a_recv, 0, 1)

    loads[4].wait()
    for j in range(2):
        value = gate_in[:, columns(j)].astype(F32)
        gate[:, columns(j)] = value / (1.0 + jnp.exp(-value))
        rows = weight[pl.ds(pl.multiple_of(ch * WIDTH + j * HALF, HALF), HALF), :]
        own_part[:, columns(j)] = dot(cot[...], rows, 1, 1)

    def send_grad(j):
        parts[j].wait_recv()
        if j == 0:
            parts[1].start()
        grad_gated = (own_part[:, columns(j)] + part_recv[j].astype(F32)).astype(BF16)
        grad_mixed = grad_gated.astype(F32) * gate[:, columns(j)]
        b_send[slots(j)] = grad_mixed.reshape(CHIPS, ROWS, HALF).astype(BF16)
        spread(b_send, b_recv, 1, j)

    send_grad(0)
    share.wait_recv()
    wait_all(a_recv, recv_sem.at[0])
    mix(a_recv, m_send, False)
    give_back(m_send, a_ret, 2, a_ret_sem)
    send_grad(1)

    blocks_t[...] = blocks[0].T
    wait_all(b_recv, recv_sem.at[1])
    mix(b_recv, g_send, True)
    give_back(g_send, b_ret, 3, b_ret_sem)

    gates = [across_copy(gated.at[j], gated_other.at[j], gated_sem, j) for j in range(2)]
    for j in range(2):
        wait_all(a_ret.at[slots(j)], a_ret_sem.at[j])
        mixed = a_ret[slots(j)].astype(F32).reshape(BLOCK, HALF)
        gated[j] = (mixed * gate[:, columns(j)]).astype(BF16)
        gates[j].start()
    for j in range(2):
        rows = weight[pl.ds(pl.multiple_of(ch * WIDTH + j * HALF, HALF), HALF), :]
        if j == 0:
            total[...] = dot(gated[j], rows)
        else:
            total[...] += dot(gated[j], rows)

    for j in range(2):
        wait_all(b_ret.at[slots(j)], b_ret_sem.at[j])
        grad_first = b_ret[slots(j)].astype(F32).reshape(BLOCK, HALF).astype(BF16)
        grad_ref[:, columns(j)] = dot(blocks_t[...], grad_first).astype(BF16)

    for j in range(2):
        gates[j].wait_recv()
        rows = weight[pl.ds(pl.multiple_of((1 - ch) * WIDTH + j * HALF, HALF), HALF), :]
        if j == 0:
            total[...] += dot(gated_other[j], rows)
        else:
            result_ref[...] = (total[...] + dot(gated_other[j], rows)).astype(BF16)

    for j in range(2):
        parts[j].wait_send()
        gates[j].wait_send()
    share.wait_send()
    for k, ref in enumerate((a_send, b_send, m_send, g_send)):
        sent = ref.at[pl.ds(0, SEQ - 1)]
        wait_all(sent, send_sem.at[k])


def write_out(result, grad_in, result_hbm, grad_hbm, sems):
    copies = [
        pltpu.make_async_copy(result, result_hbm, sems.at[0]),
        pltpu.make_async_copy(grad_in, grad_hbm, sems.at[1]),
    ]
    for copy in copies:
        copy.start()
    for copy in copies:
        copy.wait()


def body(seq_in, gate_in, first_blocks, second_blocks, out_weight, cotangent):
    whole = pltpu.VMEM((BLOCK, WIDTH), BF16)
    whole_f32 = pltpu.VMEM((BLOCK, WIDTH), F32)
    halves = pltpu.VMEM((2, BLOCK, HALF), BF16)
    messages = pltpu.VMEM((SEQ, ROWS, HALF), BF16)
    wide = pltpu.VMEM((COLS, SEQ * ROWS, 128), F32)
    dma = pltpu.SemaphoreType.DMA
    out = pltpu.VMEM((BLOCK, WIDTH), BF16)
    final = jax.ShapeDtypeStruct((BLOCK, WIDTH), BF16)
    result, grad_in = pl.pallas_call(
        kernel,
        out_shape=(out, out),
        in_specs=[pl.BlockSpec(memory_space=pl.ANY)] * 6,
        out_specs=(pl.BlockSpec(memory_space=pltpu.VMEM),) * 2,
        scratch_shapes=[
            whole,
            whole,
            pltpu.VMEM((1, BLOCK, BLOCK), BF16),
            pltpu.VMEM((ROWS, SEQ, SEQ), BF16),
            pltpu.VMEM((2 * WIDTH, WIDTH), BF16),
            whole,
            whole_f32,
            whole_f32,
            halves,
            halves,
        ]
        + [messages] * 8
        + [wide, wide, halves, halves, whole_f32, pltpu.VMEM((BLOCK, BLOCK), BF16)]
        + [dma((6,)), dma((2,)), dma((4,)), dma((4,)), dma((4,)), dma((2,)), dma((2,)), dma((2,))],
        compiler_params=pltpu.CompilerParams(
            collective_id=0, has_side_effects=True, vmem_limit_bytes=60 * 2**20
        ),
        cost_estimate=pl.CostEstimate(
            flops=3_500_000_000, bytes_accessed=7_000_000, transcendentals=400_000
        ),
        name="monarch",
    )(seq_in, gate_in, first_blocks, second_blocks, out_weight, cotangent)
    return pl.pallas_call(
        write_out,
        out_shape=(final, final),
        in_specs=[pl.BlockSpec(memory_space=pl.ANY)] * 2,
        out_specs=(pl.BlockSpec(memory_space=pl.ANY),) * 2,
        scratch_shapes=[dma((2,))],
        name="write_out",
    )(
        pltpu.with_memory_space_constraint(result, pltpu.VMEM),
        pltpu.with_memory_space_constraint(grad_in, pltpu.VMEM),
    )


def solution(mesh):
    return jax.shard_map(
        body,
        mesh=mesh,
        in_specs=(
            P("seq", "ch"),
            P("seq", "ch"),
            P("seq", None, None),
            P("seq", None, None),
            P(None, "ch"),
            P("seq", "ch"),
        ),
        out_specs=(P("seq", "ch"), P("seq", "ch")),
        check_vma=False,
    )
```

```python
import jax
import jax.numpy as jnp
from jax import lax
from jax.experimental import pallas as pl
from jax.experimental.pallas import tpu as pltpu
from jax.sharding import PartitionSpec as P

MESH = pl.DeviceIdType.MESH
SEQ = 128
CHIPS = SEQ // 2
ROWS = 8
BLOCK = 512
WIDTH = 768
HALF = WIDTH // 2
COLS = HALF // 128
F32 = jnp.float32
BF16 = jnp.bfloat16


def dot(a, b, ca=1, cb=0):
    return lax.dot_general(a, b, (((ca,), (cb,)), ((), ())), preferred_element_type=F32)


def kernel(
    seq_hbm, gate_hbm, first_hbm, second_hbm, weight_hbm, cot_hbm,
    result_ref, grad_ref,
    seq, gate_in, blocks, second, weight, cot,
    gate, own_part, part_send, part_recv,
    a_send, a_recv, m_send, a_ret,
    b_send, b_recv, g_send, b_ret,
    wide, wide_out, gated, gated_other, total, blocks_t,
    load_sem, second_sem, part_sem, gated_sem, send_sem, recv_sem, a_ret_sem, b_ret_sem,
):
    me = lax.axis_index("seq")
    ch = lax.axis_index("ch")
    chip, core = me // 2, lax.rem(me, 2)
    partner = me + 1 - 2 * core
    across = {"ch": 1 - ch}
    hub = core * CHIPS + chip

    loads = [
        pltpu.make_async_copy(src, dst, load_sem.at[k])
        for k, (src, dst) in enumerate(
            [
                (first_hbm, blocks),
                (seq_hbm, seq),
                (cot_hbm, cot),
                (weight_hbm, weight),
                (gate_hbm, gate_in),
                (second_hbm, second.at[pl.ds(core * 4, 4)]),
            ]
        )
    ]
    for load in loads:
        load.start()

    barrier = pltpu.get_barrier_semaphore()

    @pl.loop(1, SEQ)
    def _(s):
        pl.semaphore_signal(
            barrier, inc=1, device_id={"seq": lax.rem(me + s, SEQ)}, device_id_type=MESH
        )

    pl.semaphore_signal(barrier, inc=1, device_id=across, device_id_type=MESH)

    def columns(j):
        return pl.ds(j * HALF, HALF)

    def slots(j):
        return pl.ds(j * CHIPS, CHIPS)

    loads[0].wait()
    loads[1].wait()
    for j in range(2):
        part = dot(blocks[0], seq[:, columns(j)])
        a_send[slots(j)] = part.reshape(CHIPS, ROWS, HALF).astype(BF16)
    loads[2].wait()
    loads[3].wait()
    for j in range(2):
        rows = weight[pl.ds(pl.multiple_of((1 - ch) * WIDTH + j * HALF, HALF), HALF), :]
        part_send[j] = dot(cot[...], rows, 1, 1).astype(BF16)
    loads[5].wait()

    pl.semaphore_wait(barrier, SEQ)

    def across_copy(src, dst, sems, j):
        return pltpu.make_async_remote_copy(
            src, dst, sems.at[j], sems.at[2 + j], device_id=across, device_id_type=MESH
        )

    def to_peer(src, dst, send, recv, peer):
        return pltpu.make_async_remote_copy(
            src, dst, send, recv, device_id={"seq": peer}, device_id_type=MESH
        )

    def spread(send, recv, k, j):
        @pl.loop(1, CHIPS, unroll=7)
        def _(s):
            t = lax.rem(chip + s, CHIPS)
            to_peer(
                send.at[j * CHIPS + t], recv.at[me], send_sem.at[k], recv_sem.at[k], 2 * t + j
            ).start()

        slot = j * CHIPS + chip

        @pl.when(core == j)
        def _():
            pltpu.make_async_copy(send.at[slot], recv.at[me], recv_sem.at[k]).start()

        @pl.when(core != j)
        def _():
            to_peer(send.at[slot], recv.at[me], send_sem.at[k], recv_sem.at[k], partner).start()

    def give_back(send, recv, k, sems):
        @pl.loop(1, CHIPS, unroll=7)
        def _(s):
            t = lax.rem(chip + s, CHIPS)
            for j in range(2):
                peer = 2 * t + j
                to_peer(send.at[peer], recv.at[hub], send_sem.at[k], sems.at[core], peer).start()

        to_peer(send.at[partner], recv.at[hub], send_sem.at[k], sems.at[core], partner).start()

        pltpu.make_async_copy(send.at[me], recv.at[hub], sems.at[core]).start()

    def wait_all(ref, sem):
        pltpu.make_async_copy(ref, ref, sem).wait()

    def mix(recv, send, back):
        for k in range(COLS):
            lanes = pl.ds(k * 128, 128)
            wide[k, pl.ds(0, SEQ * ROWS)] = recv[:, :, lanes].astype(F32).reshape(SEQ * ROWS, 128)
        for i in range(ROWS):
            at = pl.ds(i, SEQ, stride=ROWS)
            rows = [wide[k, at, :].astype(BF16) for k in range(COLS)]
            part = dot(second[i], jnp.concatenate(rows, axis=1), 0 if back else 1, 0)
            for k in range(COLS):
                wide_out[k, at, :] = part[:, k * 128 : (k + 1) * 128]
        for k in range(COLS):
            lanes = pl.ds(k * 128, 128)
            send[:, :, lanes] = wide_out[k, pl.ds(0, SEQ * ROWS)].reshape(SEQ, ROWS, 128).astype(BF16)

    share = to_peer(
        second.at[pl.ds(core * 4, 4)],
        second.at[pl.ds(core * 4, 4)],
        second_sem.at[0],
        second_sem.at[1],
        partner,
    )
    share.start()
    parts = [across_copy(part_send.at[j], part_recv.at[j], part_sem, j) for j in range(2)]
    parts[0].start()
    spread(a_send, a_recv, 0, 0)
    spread(a_send, a_recv, 0, 1)

    loads[4].wait()
    for j in range(2):
        value = gate_in[:, columns(j)].astype(F32)
        gate[:, columns(j)] = value / (1.0 + jnp.exp(-value))
        rows = weight[pl.ds(pl.multiple_of(ch * WIDTH + j * HALF, HALF), HALF), :]
        own_part[:, columns(j)] = dot(cot[...], rows, 1, 1)

    def send_grad(j):
        parts[j].wait_recv()
        if j == 0:
            parts[1].start()
        grad_gated = (own_part[:, columns(j)] + part_recv[j].astype(F32)).astype(BF16)
        grad_mixed = grad_gated.astype(F32) * gate[:, columns(j)]
        b_send[slots(j)] = grad_mixed.reshape(CHIPS, ROWS, HALF).astype(BF16)
        spread(b_send, b_recv, 1, j)

    send_grad(0)
    share.wait_recv()
    wait_all(a_recv, recv_sem.at[0])
    mix(a_recv, m_send, False)
    give_back(m_send, a_ret, 2, a_ret_sem)
    send_grad(1)

    blocks_t[...] = blocks[0].T
    wait_all(b_recv, recv_sem.at[1])
    mix(b_recv, g_send, True)
    give_back(g_send, b_ret, 3, b_ret_sem)

    gates = [across_copy(gated.at[j], gated_other.at[j], gated_sem, j) for j in range(2)]
    for j in range(2):
        wait_all(a_ret.at[slots(j)], a_ret_sem.at[j])
        mixed = a_ret[slots(j)].astype(F32).reshape(BLOCK, HALF)
        gated[j] = (mixed * gate[:, columns(j)]).astype(BF16)
        gates[j].start()
    for j in range(2):
        rows = weight[pl.ds(pl.multiple_of(ch * WIDTH + j * HALF, HALF), HALF), :]
        if j == 0:
            total[...] = dot(gated[j], rows)
        else:
            total[...] += dot(gated[j], rows)

    for j in range(2):
        wait_all(b_ret.at[slots(j)], b_ret_sem.at[j])
        grad_first = b_ret[slots(j)].astype(F32).reshape(BLOCK, HALF).astype(BF16)
        grad_ref[:, columns(j)] = dot(blocks_t[...], grad_first).astype(BF16)

    for j in range(2):
        gates[j].wait_recv()
        rows = weight[pl.ds(pl.multiple_of((1 - ch) * WIDTH + j * HALF, HALF), HALF), :]
        if j == 0:
            total[...] += dot(gated_other[j], rows)
        else:
            result_ref[...] = (total[...] + dot(gated_other[j], rows)).astype(BF16)

    for j in range(2):
        parts[j].wait_send()
        gates[j].wait_send()
    share.wait_send()
    for k, ref in enumerate((a_send, b_send, m_send, g_send)):
        sent = ref.at[pl.ds(0, SEQ - 1)]
        wait_all(sent, send_sem.at[k])


def write_out(result, grad_in, result_hbm, grad_hbm, sems):
    copies = [
        pltpu.make_async_copy(result, result_hbm, sems.at[0]),
        pltpu.make_async_copy(grad_in, grad_hbm, sems.at[1]),
    ]
    for copy in copies:
        copy.start()
    for copy in copies:
        copy.wait()


def body(seq_in, gate_in, first_blocks, second_blocks, out_weight, cotangent):
    whole = pltpu.VMEM((BLOCK, WIDTH), BF16)
    whole_f32 = pltpu.VMEM((BLOCK, WIDTH), F32)
    halves = pltpu.VMEM((2, BLOCK, HALF), BF16)
    messages = pltpu.VMEM((SEQ, ROWS, HALF), BF16)
    wide = pltpu.VMEM((COLS, SEQ * ROWS + ROWS, 128), F32)
    dma = pltpu.SemaphoreType.DMA
    out = pltpu.VMEM((BLOCK, WIDTH), BF16)
    final = jax.ShapeDtypeStruct((BLOCK, WIDTH), BF16)
    result, grad_in = pl.pallas_call(
        kernel,
        out_shape=(out, out),
        in_specs=[pl.BlockSpec(memory_space=pl.ANY)] * 6,
        out_specs=(pl.BlockSpec(memory_space=pltpu.VMEM),) * 2,
        scratch_shapes=[
            whole,
            whole,
            pltpu.VMEM((1, BLOCK, BLOCK), BF16),
            pltpu.VMEM((ROWS, SEQ, SEQ), BF16),
            pltpu.VMEM((2 * WIDTH, WIDTH), BF16),
            whole,
            whole_f32,
            whole_f32,
            halves,
            halves,
        ]
        + [messages] * 8
        + [wide, wide, halves, halves, whole_f32, pltpu.VMEM((BLOCK, BLOCK), BF16)]
        + [dma((6,)), dma((2,)), dma((4,)), dma((4,)), dma((4,)), dma((2,)), dma((2,)), dma((2,))],
        compiler_params=pltpu.CompilerParams(
            collective_id=0, has_side_effects=True, vmem_limit_bytes=60 * 2**20
        ),
        cost_estimate=pl.CostEstimate(
            flops=3_500_000_000, bytes_accessed=7_000_000, transcendentals=400_000
        ),
        name="monarch",
    )(seq_in, gate_in, first_blocks, second_blocks, out_weight, cotangent)
    return pl.pallas_call(
        write_out,
        out_shape=(final, final),
        in_specs=[pl.BlockSpec(memory_space=pl.ANY)] * 2,
        out_specs=(pl.BlockSpec(memory_space=pl.ANY),) * 2,
        scratch_shapes=[dma((2,))],
        name="write_out",
    )(
        pltpu.with_memory_space_constraint(result, pltpu.VMEM),
        pltpu.with_memory_space_constraint(grad_in, pltpu.VMEM),
    )


def solution(mesh):
    return jax.shard_map(
        body,
        mesh=mesh,
        in_specs=(
            P("seq", "ch"),
            P("seq", "ch"),
            P("seq", None, None),
            P("seq", None, None),
            P(None, "ch"),
            P("seq", "ch"),
        ),
        out_specs=(P("seq", "ch"), P("seq", "ch")),
        check_vma=False,
    )
```

```python
import jax
import jax.numpy as jnp
from jax import lax
from jax.experimental import pallas as pl
from jax.experimental.pallas import tpu as pltpu
from jax.sharding import PartitionSpec as P

MESH = pl.DeviceIdType.MESH
SEQ = 128
CHIPS = SEQ // 2
ROWS = 8
BLOCK = 512
WIDTH = 768
HALF = WIDTH // 2
COLS = HALF // 128
F32 = jnp.float32
BF16 = jnp.bfloat16


def dot(a, b, ca=1, cb=0):
    return lax.dot_general(a, b, (((ca,), (cb,)), ((), ())), preferred_element_type=F32)


def kernel(
    seq_hbm, gate_hbm, first_hbm, second_hbm, weight_hbm, cot_hbm,
    result_ref, grad_ref,
    seq, gate_in, blocks, second, weight, cot,
    gate, own_part, part_send, part_recv,
    a_send, a_recv, m_send, a_ret,
    b_send, b_recv, g_send, b_ret,
    wide, wide_out, gated, gated_other, total, blocks_t,
    load_sem, second_sem, part_sem, gated_sem, send_sem, recv_sem, a_ret_sem, b_ret_sem,
):
    me = lax.axis_index("seq")
    ch = lax.axis_index("ch")
    chip, core = me // 2, lax.rem(me, 2)
    partner = me + 1 - 2 * core
    across = {"ch": 1 - ch}
    hub = core * CHIPS + chip

    barrier = pltpu.get_barrier_semaphore()

    @pl.loop(1, SEQ - 1, unroll=6)
    def _(s):
        pl.semaphore_signal(
            barrier, inc=1, device_id={"seq": lax.rem(me + s, SEQ)}, device_id_type=MESH
        )

    pl.semaphore_signal(
        barrier, inc=1, device_id={"seq": lax.rem(me + SEQ - 1, SEQ)}, device_id_type=MESH
    )
    pl.semaphore_signal(barrier, inc=1, device_id=across, device_id_type=MESH)

    loads = [
        pltpu.make_async_copy(src, dst, load_sem.at[k])
        for k, (src, dst) in enumerate(
            [
                (first_hbm, blocks),
                (seq_hbm, seq),
                (cot_hbm, cot),
                (weight_hbm, weight),
                (gate_hbm, gate_in),
                (second_hbm, second.at[pl.ds(core * 4, 4)]),
            ]
        )
    ]
    for load in loads:
        load.start()

    def columns(j):
        return pl.ds(j * HALF, HALF)

    def slots(j):
        return pl.ds(j * CHIPS, CHIPS)

    loads[0].wait()
    loads[1].wait()
    for j in range(2):
        part = dot(blocks[0], seq[:, columns(j)])
        a_send[slots(j)] = part.reshape(CHIPS, ROWS, HALF).astype(BF16)
    loads[2].wait()
    loads[3].wait()
    for j in range(2):
        rows = weight[pl.ds(pl.multiple_of((1 - ch) * WIDTH + j * HALF, HALF), HALF), :]
        part_send[j] = dot(cot[...], rows, 1, 1).astype(BF16)
    loads[5].wait()

    pl.semaphore_wait(barrier, SEQ)

    def across_copy(src, dst, sems, j):
        return pltpu.make_async_remote_copy(
            src, dst, sems.at[j], sems.at[2 + j], device_id=across, device_id_type=MESH
        )

    def to_peer(src, dst, send, recv, peer):
        return pltpu.make_async_remote_copy(
            src, dst, send, recv, device_id={"seq": peer}, device_id_type=MESH
        )

    def spread(send, recv, k, j):
        @pl.loop(1, CHIPS, unroll=7)
        def _(s):
            t = lax.rem(chip + s, CHIPS)
            to_peer(
                send.at[j * CHIPS + t], recv.at[me], send_sem.at[k], recv_sem.at[k], 2 * t + j
            ).start()

        slot = j * CHIPS + chip

        @pl.when(core == j)
        def _():
            pltpu.make_async_copy(send.at[slot], recv.at[me], recv_sem.at[k]).start()

        @pl.when(core != j)
        def _():
            to_peer(send.at[slot], recv.at[me], send_sem.at[k], recv_sem.at[k], partner).start()

    def give_back(send, recv, k, sems):
        @pl.loop(1, CHIPS, unroll=7)
        def _(s):
            t = lax.rem(chip + s, CHIPS)
            for j in range(2):
                peer = 2 * t + j
                to_peer(send.at[peer], recv.at[hub], send_sem.at[k], sems.at[core], peer).start()

        to_peer(send.at[partner], recv.at[hub], send_sem.at[k], sems.at[core], partner).start()

        pltpu.make_async_copy(send.at[me], recv.at[hub], sems.at[core]).start()

    def wait_all(ref, sem):
        pltpu.make_async_copy(ref, ref, sem).wait()

    def mix(recv, send, back):
        for k in range(COLS):
            lanes = pl.ds(k * 128, 128)
            wide[k, pl.ds(0, SEQ * ROWS)] = recv[:, :, lanes].astype(F32).reshape(SEQ * ROWS, 128)
        for i in range(ROWS):
            at = pl.ds(i, SEQ, stride=ROWS)
            rows = [wide[k, at, :].astype(BF16) for k in range(COLS)]
            part = dot(second[i], jnp.concatenate(rows, axis=1), 0 if back else 1, 0)
            for k in range(COLS):
                wide_out[k, at, :] = part[:, k * 128 : (k + 1) * 128]
        for k in range(COLS):
            lanes = pl.ds(k * 128, 128)
            send[:, :, lanes] = wide_out[k, pl.ds(0, SEQ * ROWS)].reshape(SEQ, ROWS, 128).astype(BF16)

    share = to_peer(
        second.at[pl.ds(core * 4, 4)],
        second.at[pl.ds(core * 4, 4)],
        second_sem.at[0],
        second_sem.at[1],
        partner,
    )
    share.start()
    parts = [across_copy(part_send.at[j], part_recv.at[j], part_sem, j) for j in range(2)]
    parts[0].start()
    spread(a_send, a_recv, 0, 0)
    spread(a_send, a_recv, 0, 1)

    loads[4].wait()
    for j in range(2):
        value = gate_in[:, columns(j)].astype(F32)
        gate[:, columns(j)] = value / (1.0 + jnp.exp(-value))
        rows = weight[pl.ds(pl.multiple_of(ch * WIDTH + j * HALF, HALF), HALF), :]
        own_part[:, columns(j)] = dot(cot[...], rows, 1, 1)

    def send_grad(j):
        parts[j].wait_recv()
        if j == 0:
            parts[1].start()
        grad_gated = (own_part[:, columns(j)] + part_recv[j].astype(F32)).astype(BF16)
        grad_mixed = grad_gated.astype(F32) * gate[:, columns(j)]
        b_send[slots(j)] = grad_mixed.reshape(CHIPS, ROWS, HALF).astype(BF16)
        spread(b_send, b_recv, 1, j)

    send_grad(0)
    share.wait_recv()
    wait_all(a_recv, recv_sem.at[0])
    mix(a_recv, m_send, False)
    give_back(m_send, a_ret, 2, a_ret_sem)
    send_grad(1)

    blocks_t[...] = blocks[0].T
    wait_all(b_recv, recv_sem.at[1])
    mix(b_recv, g_send, True)
    give_back(g_send, b_ret, 3, b_ret_sem)

    gates = [across_copy(gated.at[j], gated_other.at[j], gated_sem, j) for j in range(2)]
    for j in range(2):
        wait_all(a_ret.at[slots(j)], a_ret_sem.at[j])
        mixed = a_ret[slots(j)].astype(F32).reshape(BLOCK, HALF)
        gated[j] = (mixed * gate[:, columns(j)]).astype(BF16)
        gates[j].start()
    for j in range(2):
        rows = weight[pl.ds(pl.multiple_of(ch * WIDTH + j * HALF, HALF), HALF), :]
        if j == 0:
            total[...] = dot(gated[j], rows)
        else:
            total[...] += dot(gated[j], rows)

    for j in range(2):
        wait_all(b_ret.at[slots(j)], b_ret_sem.at[j])
        grad_first = b_ret[slots(j)].astype(F32).reshape(BLOCK, HALF).astype(BF16)
        grad_ref[:, columns(j)] = dot(blocks_t[...], grad_first).astype(BF16)

    for j in range(2):
        gates[j].wait_recv()
        rows = weight[pl.ds(pl.multiple_of((1 - ch) * WIDTH + j * HALF, HALF), HALF), :]
        if j == 0:
            total[...] += dot(gated_other[j], rows)
        else:
            result_ref[...] = (total[...] + dot(gated_other[j], rows)).astype(BF16)

    for j in range(2):
        parts[j].wait_send()
        gates[j].wait_send()
    share.wait_send()
    for k, ref in enumerate((a_send, b_send, m_send, g_send)):
        sent = ref.at[pl.ds(0, SEQ - 1)]
        wait_all(sent, send_sem.at[k])


def write_out(result, grad_in, result_hbm, grad_hbm, sems):
    copies = [
        pltpu.make_async_copy(result, result_hbm, sems.at[0]),
        pltpu.make_async_copy(grad_in, grad_hbm, sems.at[1]),
    ]
    for copy in copies:
        copy.start()
    for copy in copies:
        copy.wait()


def body(seq_in, gate_in, first_blocks, second_blocks, out_weight, cotangent):
    whole = pltpu.VMEM((BLOCK, WIDTH), BF16)
    whole_f32 = pltpu.VMEM((BLOCK, WIDTH), F32)
    halves = pltpu.VMEM((2, BLOCK, HALF), BF16)
    messages = pltpu.VMEM((SEQ, ROWS, HALF), BF16)
    wide = pltpu.VMEM((COLS, SEQ * ROWS + ROWS, 128), F32)
    dma = pltpu.SemaphoreType.DMA
    out = pltpu.VMEM((BLOCK, WIDTH), BF16)
    final = jax.ShapeDtypeStruct((BLOCK, WIDTH), BF16)
    result, grad_in = pl.pallas_call(
        kernel,
        out_shape=(out, out),
        in_specs=[pl.BlockSpec(memory_space=pl.ANY)] * 6,
        out_specs=(pl.BlockSpec(memory_space=pltpu.VMEM),) * 2,
        scratch_shapes=[
            whole,
            whole,
            pltpu.VMEM((1, BLOCK, BLOCK), BF16),
            pltpu.VMEM((ROWS, SEQ, SEQ), BF16),
            pltpu.VMEM((2 * WIDTH, WIDTH), BF16),
            whole,
            whole_f32,
            whole_f32,
            halves,
            halves,
        ]
        + [messages] * 8
        + [wide, wide, halves, halves, whole_f32, pltpu.VMEM((BLOCK, BLOCK), BF16)]
        + [dma((6,)), dma((2,)), dma((4,)), dma((4,)), dma((4,)), dma((2,)), dma((2,)), dma((2,))],
        compiler_params=pltpu.CompilerParams(
            collective_id=0, has_side_effects=True, vmem_limit_bytes=60 * 2**20
        ),
        cost_estimate=pl.CostEstimate(
            flops=3_500_000_000, bytes_accessed=7_000_000, transcendentals=400_000
        ),
        name="monarch",
    )(seq_in, gate_in, first_blocks, second_blocks, out_weight, cotangent)
    return pl.pallas_call(
        write_out,
        out_shape=(final, final),
        in_specs=[pl.BlockSpec(memory_space=pl.ANY)] * 2,
        out_specs=(pl.BlockSpec(memory_space=pl.ANY),) * 2,
        scratch_shapes=[dma((2,))],
        name="write_out",
    )(
        pltpu.with_memory_space_constraint(result, pltpu.VMEM),
        pltpu.with_memory_space_constraint(grad_in, pltpu.VMEM),
    )


def solution(mesh):
    return jax.shard_map(
        body,
        mesh=mesh,
        in_specs=(
            P("seq", "ch"),
            P("seq", "ch"),
            P("seq", None, None),
            P("seq", None, None),
            P(None, "ch"),
            P("seq", "ch"),
        ),
        out_specs=(P("seq", "ch"), P("seq", "ch")),
        check_vma=False,
    )
```
